32 devices in a mesh: wave: 2 (over y), tile: 16 (over z, x, core).
Axes of the slice: x: 2, y: 2, z: 4, core: 2. Of those that a mesh axis runs over, the one named last changes fastest.
Arguments:
- coefficients: bfloat16 [256, 256, 4096], P('tile', 'wave'), may hold values from -2.09375 to 2.09375
- profile_basis: bfloat16 [4096, 512], replicated, may hold values from -0.26367188 to 0.26367188
- point_spread: bfloat16 [17, 17], replicated, may hold values from 0.0009994507 to 0.0099487305
- observed: bfloat16 [512, 256, 256], P(None, 'tile', 'wave'), may hold values from -6 to 6
Outputs:
- coef_grad: bfloat16 [256, 256, 4096], P('tile', 'wave')
The draws below stay inside these ranges and needn't reach their ends.
All inputs are finite; a program needn't handle non-finite values.
Results may differ from the reference program's by a relative error of at most 0.0058.
Values may be sent and summed in bfloat16 or wider, within the bound.
A program may use at most 192 MiB of HBM per device.

```python
import math
import jax
import jax.numpy as jnp
from jax import lax

PROFILES = 4096
WAVES = 512
COLS = 256
PSF = 17
ROWS = 256


def levels(key, extent, split, smallest, high):
    factor_of = 1.0
    for position, parts in split:
        steps = jax.random.uniform(jax.random.fold_in(jax.random.fold_in(key, 6), position), (parts,), jnp.float32, smallest / len(split), high / len(split))
        factor_of = factor_of * jnp.repeat(jnp.exp(steps), extent[position] // parts).reshape((-1,) + (1,) * (len(extent) - 1 - position))
    return factor_of


def gaussian(stream_key, dims, width, reach, split=(), kind=jnp.bfloat16):
    gain = levels(stream_key, dims, split, -0.22, 0.18) if split else 1.0
    array = jax.random.normal(stream_key, dims, jnp.float32) * width * gain
    return jnp.minimum(jnp.maximum(array, -reach), reach).astype(kind)


def setup_inputs(seed: int = 0) -> dict:
    splits = jax.random.split(jax.random.key(seed), 5)
    return {
        "coefficients": gaussian(splits[0], (ROWS, COLS, PROFILES), 0.35, 2.09375, ((0, 16), (1, 2))),
        "profile_basis": gaussian(splits[1], (PROFILES, WAVES), (WAVES ** -0.5), 0.26367188),
        "point_spread": jnp.clip(jnp.exp(jax.random.uniform(splits[2], (PSF, PSF), jnp.float32, math.log(0.0009994507), math.log(0.0099487305))), 0.0009994507, 0.0099487305).astype(jnp.bfloat16),
        "observed": gaussian(splits[3], (WAVES, ROWS, COLS), 1.0, 6.0, ((1, 16), (2, 2))),
    }


def blur_planes(field, kernel):
    half_width = kernel.shape[0] // 2
    result = lax.conv_general_dilated(field[:, None], kernel[None, None], (1, 1), ((half_width, half_width), (half_width, half_width)), precision=lax.Precision.HIGHEST)
    return result[:, 0]


def reference(coefficients, profile_basis, point_spread, observed):
    opacity = jnp.dot(coefficients.reshape(-1, PROFILES), profile_basis, preferred_element_type=jnp.float32)
    spectra = jnp.exp(-opacity).astype(jnp.bfloat16).reshape(ROWS, COLS, WAVES).transpose(2, 0, 1)
    kernel_f = point_spread.astype(jnp.float32)
    blurred = blur_planes(spectra.astype(jnp.float32), kernel_f)
    residual = (blurred - observed.astype(jnp.float32)).astype(jnp.bfloat16)
    adjoint_field = blur_planes(residual.astype(jnp.float32), kernel_f[::-1, ::-1])
    tau_grad = (-spectra.astype(jnp.float32) * adjoint_field).astype(jnp.bfloat16)
    pixel_grad = tau_grad.transpose(1, 2, 0).reshape(-1, WAVES)
    coef_grad = jnp.dot(pixel_grad, profile_basis.T, preferred_element_type=jnp.float32)
    return coef_grad.astype(jnp.bfloat16).reshape(ROWS, COLS, PROFILES)
```

```python
import functools

import jax
import jax.numpy as jnp
from jax import lax
from jax.experimental import pallas as pl
from jax.experimental.pallas import tpu as pltpu
from jax.sharding import PartitionSpec as P

MESH = pl.DeviceIdType.MESH
EDGE = 16
PATCH = 16
CHUNKS = 2
TILE_ROWS = 2
COL_RIGHT, COL_LEFT, ROW_UP, ROW_DOWN, UP_LEFT, UP_RIGHT, DOWN_LEFT, DOWN_RIGHT = range(8)


def stencil_matrix(psf_ref, out_ref, half, adjoint):
    width_in = PATCH + 2 * EDGE
    rows_in = PATCH + 2 * half
    total = rows_in * width_in
    psf = psf_ref[...]
    taps = 2 * half + 1
    lane = lax.broadcasted_iota(jnp.int32, (psf.shape[0], total), 1)
    height = jnp.zeros_like(lane)
    for m in range(1, rows_in):
        height = height + jnp.where(lane >= m * width_in, 1, 0)
    tap = lax.broadcasted_iota(jnp.int32, (psf.shape[0], total), 0)
    wanted = (taps - 1) - tap if adjoint else tap
    onehot = jnp.where(wanted == height, 1.0, 0.0).astype(jnp.bfloat16)
    spread = lax.dot_general(
        psf, onehot, (((0,), (0,)), ((), ())), preferred_element_type=jnp.float32
    )
    lane = lax.broadcasted_iota(jnp.int32, (PATCH, total), 1)
    height = jnp.zeros_like(lane)
    for m in range(1, rows_in):
        height = height + jnp.where(lane >= m * width_in, 1, 0)
    shift = (lane - height * width_in - (EDGE - half)
             - lax.broadcasted_iota(jnp.int32, (PATCH, total), 0))
    base = jnp.zeros((PATCH, total), jnp.float32)
    for b in range(taps):
        at = taps - 1 - b if adjoint else b
        base = base + jnp.where(shift == at, spread[b:b + 1, :], 0.0)
    for r in range(PATCH):
        rolled = base if r == 0 else pltpu.roll(base, r * width_in, 1)
        out_ref[r * PATCH:(r + 1) * PATCH, :] = rolled.astype(jnp.bfloat16)


def kernel(half, n_tile, n_wave, coef_ref, basis_hbm, psf_ref, obs_hbm, tau_ref,
           coef, basis, obs, spec, resid, fwd, adj,
           coef_sem, load_sem, send_sem, recv_sem):
    rows = spec.shape[0] - 2 * half
    cols = spec.shape[1] - 2 * EDGE
    waves = spec.shape[2]
    width = waves // CHUNKS
    tile = lax.axis_index("tile")
    wave = lax.axis_index("wave")
    has = {
        "up": tile > 0, "down": tile < n_tile - 1,
        "left": wave > 0, "right": wave < n_wave - 1,
    }
    device = {
        "up": {"tile": tile - 1}, "down": {"tile": tile + 1},
        "left": {"wave": wave - 1}, "right": {"wave": wave + 1},
    }
    odd = lax.rem(tile, 2)
    steps = rows // TILE_ROWS
    per_half = steps // 2

    def tile_at(t):
        return lax.rem(t + odd * per_half, steps)

    def coef_copy(t):
        at = tile_at(t) * TILE_ROWS
        return pltpu.make_async_copy(
            coef_ref.at[pl.ds(at, TILE_ROWS)], coef.at[pl.ds(at, TILE_ROWS)], coef_sem.at[t]
        )

    basis_copy = pltpu.make_async_copy(basis_hbm, basis, load_sem.at[0])
    obs_copy = pltpu.make_async_copy(obs_hbm, obs, load_sem.at[1])
    basis_copy.start()
    for t in range(steps):
        coef_copy(t).start()
    obs_copy.start()

    barrier = pltpu.get_barrier_semaphore()
    for side in has:
        @pl.when(has[side])
        def _(side=side):
            pl.semaphore_signal(barrier, inc=1, device_id=device[side], device_id_type=MESH)

    for field in (spec, resid):
        @pl.when(jnp.logical_not(has["up"]))
        def _(field=field):
            field[0:half] = jnp.zeros((half,) + field.shape[1:], field.dtype)

        @pl.when(jnp.logical_not(has["down"]))
        def _(field=field):
            field[half + rows:] = jnp.zeros((half,) + field.shape[1:], field.dtype)

        @pl.when(jnp.logical_not(has["left"]))
        def _(field=field):
            field[half:half + rows, 0:EDGE] = jnp.zeros((rows, EDGE, waves), field.dtype)

        @pl.when(jnp.logical_not(has["right"]))
        def _(field=field):
            field[half:half + rows, EDGE + cols:] = jnp.zeros((rows, EDGE, waves), field.dtype)

    peers = jnp.int32(0)
    for side in has:
        peers = peers + jnp.where(has[side], 1, 0)
    pl.semaphore_wait(barrier, peers)

    top, low = half, rows
    near = rows + half

    places = {
        COL_RIGHT: ("right", "left", (half, rows), cols, 0),
        COL_LEFT: ("left", "right", (half, rows), EDGE, EDGE + cols),
        ROW_UP: ("up", "down", (top, near), EDGE, EDGE),
        ROW_DOWN: ("down", "up", (low, 0), EDGE, EDGE),
        UP_LEFT: ("up", "down", (top, near), 0, 0),
        UP_RIGHT: ("up", "down", (top, near), EDGE + cols, EDGE + cols),
        DOWN_LEFT: ("down", "up", (low, 0), 0, 0),
        DOWN_RIGHT: ("down", "up", (low, 0), EDGE + cols, EDGE + cols),
    }

    def copy(which, chunk, kind):
        field = (spec, resid)[which]
        side, _, span, source, target = places[kind]
        lanes = pl.ds(chunk * width, width)
        if kind in (COL_RIGHT, COL_LEFT):
            src = field.at[pl.ds(half, rows), pl.ds(source, EDGE), lanes]
            dst = field.at[pl.ds(half, rows), pl.ds(target, EDGE), lanes]
        else:
            size = cols if kind in (ROW_UP, ROW_DOWN) else EDGE
            src = field.at[pl.ds(span[0], half), pl.ds(source, size), lanes]
            dst = field.at[pl.ds(span[1], half), pl.ds(target, size), lanes]
        return pltpu.make_async_remote_copy(
            src_ref=src, dst_ref=dst,
            send_sem=send_sem.at[which, chunk, kind],
            recv_sem=recv_sem.at[which, chunk, kind],
            device_id=device[side], device_id_type=MESH,
        )

    def start(which, chunk, kinds):
        for kind in kinds:
            @pl.when(has[places[kind][0]])
            def _(kind=kind):
                copy(which, chunk, kind).start()

    def arrive(which, chunk, kinds):
        for kind in kinds:
            @pl.when(has[places[kind][1]])
            def _(kind=kind):
                copy(which, chunk, kind).wait_recv()

    corners = (UP_LEFT, UP_RIGHT, DOWN_LEFT, DOWN_RIGHT)

    basis_copy.wait()
    for part in range(2):
        for chunk in range(CHUNKS):
            lanes = pl.ds(chunk * width, width)
            for s in range(per_half):
                if chunk == 0:
                    coef_copy(part * per_half + s).wait()

            @pl.loop(0, per_half)
            def _(s, part=part, lanes=lanes):
                at = tile_at(part * per_half + s) * TILE_ROWS
                block = coef[pl.ds(at, TILE_ROWS)].reshape(TILE_ROWS * cols, coef.shape[2])
                opacity = jnp.dot(block, basis[:, lanes], preferred_element_type=jnp.float32)
                spec[pl.ds(half + at, TILE_ROWS), EDGE:EDGE + cols, lanes] = (
                    jnp.exp(-opacity).astype(jnp.bfloat16).reshape(TILE_ROWS, cols, width)
                )

            upper = odd if part == 1 else 1 - odd

            @pl.when(jnp.logical_and(upper == 1, has["up"]))
            def _(chunk=chunk):
                copy(0, chunk, ROW_UP).start()

            @pl.when(jnp.logical_and(upper == 0, has["down"]))
            def _(chunk=chunk):
                copy(0, chunk, ROW_DOWN).start()

            if part == 1:
                start(0, chunk, (COL_RIGHT, COL_LEFT))

    stencil_matrix(psf_ref, fwd, half, False)
    stencil_matrix(psf_ref, adj, half, True)
    for chunk in range(CHUNKS):
        arrive(0, chunk, (COL_RIGHT, COL_LEFT))
        start(0, chunk, corners)
    obs_copy.wait()

    def window(field, i, lanes):
        patch = field[:, pl.ds(i * PATCH, PATCH + 2 * EDGE), lanes]
        return patch.reshape(patch.shape[0] * patch.shape[1], width)

    for chunk in range(CHUNKS):
        lanes = pl.ds(chunk * width, width)
        arrive(0, chunk, (ROW_UP, ROW_DOWN) + corners)

        @pl.loop(0, cols // PATCH)
        def _(i, lanes=lanes):
            blurred = jnp.dot(fwd[...], window(spec, i, lanes), preferred_element_type=jnp.float32)
            seen = obs[:, pl.ds(i * PATCH, PATCH), lanes].astype(jnp.float32)
            resid[half:half + rows, pl.ds(EDGE + i * PATCH, PATCH), lanes] = (
                blurred.reshape(rows, PATCH, width) - seen
            ).astype(jnp.bfloat16)

        start(1, chunk, (COL_RIGHT, COL_LEFT, ROW_UP, ROW_DOWN))
        arrive(1, chunk, (COL_RIGHT, COL_LEFT))
        start(1, chunk, corners)

    for chunk in range(CHUNKS):
        lanes = pl.ds(chunk * width, width)
        arrive(1, chunk, (ROW_UP, ROW_DOWN) + corners)

        @pl.loop(0, cols // PATCH)
        def _(i, lanes=lanes):
            field = jnp.dot(adj[...], window(resid, i, lanes), preferred_element_type=jnp.float32)
            own = spec[half:half + rows, pl.ds(EDGE + i * PATCH, PATCH), lanes].astype(jnp.float32)
            tau_ref[:, pl.ds(i * PATCH, PATCH), lanes] = (
                -own * field.reshape(rows, PATCH, width)
            ).astype(jnp.bfloat16)

    for which in range(2):
        for chunk in range(CHUNKS):
            for kind in places:
                @pl.when(has[places[kind][0]])
                def _(which=which, chunk=chunk, kind=kind):
                    copy(which, chunk, kind).wait_send()


def shards(n_tile, n_wave, coefficients, profile_basis, point_spread, observed):
    rows, cols, profiles = coefficients.shape
    waves = profile_basis.shape[1]
    half = point_spread.shape[0] // 2
    psf = jnp.pad(point_spread, ((0, 32 - point_spread.shape[0]), (0, 128 - point_spread.shape[1])))
    seen = observed.transpose(1, 2, 0)
    padded = (rows + 2 * half, cols + 2 * EDGE, waves)
    table = (PATCH * PATCH, (PATCH + 2 * half) * (PATCH + 2 * EDGE))
    vmem = pl.BlockSpec(memory_space=pltpu.VMEM)
    hbm = pl.BlockSpec(memory_space=pl.ANY)
    tau = pl.pallas_call(
        functools.partial(kernel, half, n_tile, n_wave),
        out_shape=jax.ShapeDtypeStruct((rows, cols, waves), jnp.bfloat16),
        in_specs=[hbm, hbm, vmem, hbm],
        out_specs=vmem,
        scratch_shapes=[
            pltpu.VMEM(coefficients.shape, jnp.bfloat16),
            pltpu.VMEM(profile_basis.shape, jnp.bfloat16),
            pltpu.VMEM(seen.shape, jnp.bfloat16),
            pltpu.VMEM(padded, jnp.bfloat16),
            pltpu.VMEM(padded, jnp.bfloat16),
            pltpu.VMEM(table, jnp.bfloat16),
            pltpu.VMEM(table, jnp.bfloat16),
            pltpu.SemaphoreType.DMA((rows // TILE_ROWS,)),
            pltpu.SemaphoreType.DMA((2,)),
            pltpu.SemaphoreType.DMA((2, CHUNKS, 8)),
            pltpu.SemaphoreType.DMA((2, CHUNKS, 8)),
        ],
        compiler_params=pltpu.CompilerParams(
            collective_id=0, has_side_effects=True, vmem_limit_bytes=56 * 1024 * 1024
        ),
    )(coefficients, profile_basis, psf, seen)
    grad = jnp.dot(
        tau.reshape(rows * cols, waves), profile_basis.T, preferred_element_type=jnp.float32
    )
    return grad.astype(jnp.bfloat16).reshape(rows, cols, profiles)


def solution(mesh):
    placed = (P("tile", "wave", None), P(), P(), P(None, "tile", "wave"))
    return jax.shard_map(
        functools.partial(shards, mesh.shape["tile"], mesh.shape["wave"]),
        mesh=mesh, in_specs=placed, out_specs=P("tile", "wave", None), check_vma=False,
    )
```

```python
import functools

import jax
import jax.numpy as jnp
from jax import lax
from jax.experimental import pallas as pl
from jax.experimental.pallas import tpu as pltpu
from jax.sharding import PartitionSpec as P

MESH = pl.DeviceIdType.MESH
EDGE = 16
PATCH = 16
CHUNKS = 2
TILE_ROWS = 2
COL_RIGHT, COL_LEFT, ROW_UP, ROW_DOWN, UP_LEFT, UP_RIGHT, DOWN_LEFT, DOWN_RIGHT = range(8)


def stencil_matrix(psf_ref, out_ref, half, adjoint):
    width_in = PATCH + 2 * EDGE
    rows_in = PATCH + 2 * half
    total = rows_in * width_in
    psf = psf_ref[...]
    taps = 2 * half + 1
    lane = lax.broadcasted_iota(jnp.int32, (psf.shape[0], total), 1)
    height = jnp.zeros_like(lane)
    for m in range(1, rows_in):
        height = height + jnp.where(lane >= m * width_in, 1, 0)
    tap = lax.broadcasted_iota(jnp.int32, (psf.shape[0], total), 0)
    wanted = (taps - 1) - tap if adjoint else tap
    onehot = jnp.where(wanted == height, 1.0, 0.0).astype(jnp.bfloat16)
    spread = lax.dot_general(
        psf, onehot, (((0,), (0,)), ((), ())), preferred_element_type=jnp.float32
    )
    lane = lax.broadcasted_iota(jnp.int32, (PATCH, total), 1)
    height = jnp.zeros_like(lane)
    for m in range(1, rows_in):
        height = height + jnp.where(lane >= m * width_in, 1, 0)
    shift = (lane - height * width_in - (EDGE - half)
             - lax.broadcasted_iota(jnp.int32, (PATCH, total), 0))
    base = jnp.zeros((PATCH, total), jnp.float32)
    for b in range(taps):
        at = taps - 1 - b if adjoint else b
        base = base + jnp.where(shift == at, spread[b:b + 1, :], 0.0)
    for r in range(PATCH):
        rolled = base if r == 0 else pltpu.roll(base, r * width_in, 1)
        out_ref[r * PATCH:(r + 1) * PATCH, :] = rolled.astype(jnp.bfloat16)


def kernel(half, n_tile, n_wave, coef_ref, basis_hbm, psf_ref, obs_hbm, tau_ref,
           coef, basis, obs, spec, resid, fwd, adj,
           coef_sem, load_sem, send_sem, recv_sem):
    rows = spec.shape[0] - 2 * half
    cols = spec.shape[1] - 2 * EDGE
    waves = spec.shape[2]
    width = waves // CHUNKS
    tile = lax.axis_index("tile")
    wave = lax.axis_index("wave")
    has = {
        "up": tile > 0, "down": tile < n_tile - 1,
        "left": wave > 0, "right": wave < n_wave - 1,
    }
    device = {
        "up": {"tile": tile - 1}, "down": {"tile": tile + 1},
        "left": {"wave": wave - 1}, "right": {"wave": wave + 1},
    }
    for row in ("up", "down"):
        for col in ("left", "right"):
            has[row + col] = jnp.logical_and(has[row], has[col])
            device[row + col] = {**device[row], **device[col]}
    odd = lax.rem(tile, 2)
    steps = rows // TILE_ROWS
    per_half = steps // 2

    def tile_at(t):
        return lax.rem(t + odd * per_half, steps)

    def coef_copy(t):
        at = tile_at(t) * TILE_ROWS
        return pltpu.make_async_copy(
            coef_ref.at[pl.ds(at, TILE_ROWS)], coef.at[pl.ds(at, TILE_ROWS)], coef_sem.at[t]
        )

    basis_copy = pltpu.make_async_copy(basis_hbm, basis, load_sem.at[0])
    obs_copy = pltpu.make_async_copy(obs_hbm, obs, load_sem.at[1])
    basis_copy.start()
    for t in range(steps):
        coef_copy(t).start()
    obs_copy.start()

    barrier = pltpu.get_barrier_semaphore()
    for side in has:
        @pl.when(has[side])
        def _(side=side):
            pl.semaphore_signal(barrier, inc=1, device_id=device[side], device_id_type=MESH)

    for field in (spec, resid):
        @pl.when(jnp.logical_not(has["up"]))
        def _(field=field):
            field[0:half] = jnp.zeros((half,) + field.shape[1:], field.dtype)

        @pl.when(jnp.logical_not(has["down"]))
        def _(field=field):
            field[half + rows:] = jnp.zeros((half,) + field.shape[1:], field.dtype)

        @pl.when(jnp.logical_not(has["left"]))
        def _(field=field):
            field[:, 0:EDGE] = jnp.zeros((field.shape[0], EDGE, waves), field.dtype)

        @pl.when(jnp.logical_not(has["right"]))
        def _(field=field):
            field[:, EDGE + cols:] = jnp.zeros((field.shape[0], EDGE, waves), field.dtype)

    peers = jnp.int32(0)
    for side in has:
        peers = peers + jnp.where(has[side], 1, 0)
    pl.semaphore_wait(barrier, peers)

    top, low = half, rows
    near = rows + half

    places = {
        COL_RIGHT: ("right", "left", (half, rows), cols, 0),
        COL_LEFT: ("left", "right", (half, rows), EDGE, EDGE + cols),
        ROW_UP: ("up", "down", (top, near), EDGE, EDGE),
        ROW_DOWN: ("down", "up", (low, 0), EDGE, EDGE),
        UP_LEFT: ("upleft", "downright", (top, near), EDGE, EDGE + cols),
        UP_RIGHT: ("upright", "downleft", (top, near), cols, 0),
        DOWN_LEFT: ("downleft", "upright", (low, 0), EDGE, EDGE + cols),
        DOWN_RIGHT: ("downright", "upleft", (low, 0), cols, 0),
    }

    def copy(which, chunk, kind):
        field = (spec, resid)[which]
        side, _, span, source, target = places[kind]
        lanes = pl.ds(chunk * width, width)
        if kind in (COL_RIGHT, COL_LEFT):
            src = field.at[pl.ds(half, rows), pl.ds(source, EDGE), lanes]
            dst = field.at[pl.ds(half, rows), pl.ds(target, EDGE), lanes]
        else:
            size = cols if kind in (ROW_UP, ROW_DOWN) else EDGE
            src = field.at[pl.ds(span[0], half), pl.ds(source, size), lanes]
            dst = field.at[pl.ds(span[1], half), pl.ds(target, size), lanes]
        return pltpu.make_async_remote_copy(
            src_ref=src, dst_ref=dst,
            send_sem=send_sem.at[which, chunk, kind],
            recv_sem=recv_sem.at[which, chunk, kind],
            device_id=device[side], device_id_type=MESH,
        )

    def start(which, chunk, kinds):
        for kind in kinds:
            @pl.when(has[places[kind][0]])
            def _(kind=kind):
                copy(which, chunk, kind).start()

    def arrive(which, chunk, kinds):
        for kind in kinds:
            @pl.when(has[places[kind][1]])
            def _(kind=kind):
                copy(which, chunk, kind).wait_recv()

    ups = (UP_LEFT, UP_RIGHT, ROW_UP)
    downs = (DOWN_LEFT, DOWN_RIGHT, ROW_DOWN)
    every = ups + downs + (COL_RIGHT, COL_LEFT)

    basis_copy.wait()
    for part in range(2):
        for chunk in range(CHUNKS):
            lanes = pl.ds(chunk * width, width)
            for s in range(per_half):
                if chunk == 0:
                    coef_copy(part * per_half + s).wait()

            @pl.loop(0, per_half)
            def _(s, part=part, lanes=lanes):
                at = tile_at(part * per_half + s) * TILE_ROWS
                block = coef[pl.ds(at, TILE_ROWS)].reshape(TILE_ROWS * cols, coef.shape[2])
                opacity = jnp.dot(block, basis[:, lanes], preferred_element_type=jnp.float32)
                spec[pl.ds(half + at, TILE_ROWS), EDGE:EDGE + cols, lanes] = (
                    jnp.exp(-opacity).astype(jnp.bfloat16).reshape(TILE_ROWS, cols, width)
                )

            upper = odd if part == 1 else 1 - odd
            for wanted, kinds in ((1, ups), (0, downs)):
                @pl.when(upper == wanted)
                def _(chunk=chunk, kinds=kinds):
                    start(0, chunk, kinds)

            if part == 1:
                start(0, chunk, (COL_RIGHT, COL_LEFT))

    stencil_matrix(psf_ref, fwd, half, False)
    stencil_matrix(psf_ref, adj, half, True)
    obs_copy.wait()

    def window(field, i, lanes):
        patch = field[:, pl.ds(i * PATCH, PATCH + 2 * EDGE), lanes]
        return patch.reshape(patch.shape[0] * patch.shape[1], width)

    for chunk in range(CHUNKS):
        lanes = pl.ds(chunk * width, width)
        arrive(0, chunk, every)

        @pl.loop(0, cols // PATCH)
        def _(i, lanes=lanes):
            blurred = jnp.dot(fwd[...], window(spec, i, lanes), preferred_element_type=jnp.float32)
            seen = obs[:, pl.ds(i * PATCH, PATCH), lanes].astype(jnp.float32)
            resid[half:half + rows, pl.ds(EDGE + i * PATCH, PATCH), lanes] = (
                blurred.reshape(rows, PATCH, width) - seen
            ).astype(jnp.bfloat16)

        start(1, chunk, every)

    for chunk in range(CHUNKS):
        lanes = pl.ds(chunk * width, width)
        arrive(1, chunk, every)

        @pl.loop(0, cols // PATCH)
        def _(i, lanes=lanes):
            field = jnp.dot(adj[...], window(resid, i, lanes), preferred_element_type=jnp.float32)
            own = spec[half:half + rows, pl.ds(EDGE + i * PATCH, PATCH), lanes].astype(jnp.float32)
            tau_ref[:, pl.ds(i * PATCH, PATCH), lanes] = (
                -own * field.reshape(rows, PATCH, width)
            ).astype(jnp.bfloat16)

    for which in range(2):
        for chunk in range(CHUNKS):
            for kind in places:
                @pl.when(has[places[kind][0]])
                def _(which=which, chunk=chunk, kind=kind):
                    copy(which, chunk, kind).wait_send()


def shards(n_tile, n_wave, coefficients, profile_basis, point_spread, observed):
    rows, cols, profiles = coefficients.shape
    waves = profile_basis.shape[1]
    half = point_spread.shape[0] // 2
    psf = point_spread
    seen = observed.transpose(1, 2, 0)
    padded = (rows + 2 * half, cols + 2 * EDGE, waves)
    table = (PATCH * PATCH, (PATCH + 2 * half) * (PATCH + 2 * EDGE))
    vmem = pl.BlockSpec(memory_space=pltpu.VMEM)
    hbm = pl.BlockSpec(memory_space=pl.ANY)
    tau = pl.pallas_call(
        functools.partial(kernel, half, n_tile, n_wave),
        out_shape=jax.ShapeDtypeStruct((rows, cols, waves), jnp.bfloat16),
        in_specs=[hbm, hbm, vmem, hbm],
        out_specs=vmem,
        scratch_shapes=[
            pltpu.VMEM(coefficients.shape, jnp.bfloat16),
            pltpu.VMEM(profile_basis.shape, jnp.bfloat16),
            pltpu.VMEM(seen.shape, jnp.bfloat16),
            pltpu.VMEM(padded, jnp.bfloat16),
            pltpu.VMEM(padded, jnp.bfloat16),
            pltpu.VMEM(table, jnp.bfloat16),
            pltpu.VMEM(table, jnp.bfloat16),
            pltpu.SemaphoreType.DMA((rows // TILE_ROWS,)),
            pltpu.SemaphoreType.DMA((2,)),
            pltpu.SemaphoreType.DMA((2, CHUNKS, 8)),
            pltpu.SemaphoreType.DMA((2, CHUNKS, 8)),
        ],
        compiler_params=pltpu.CompilerParams(
            collective_id=0, has_side_effects=True, vmem_limit_bytes=56 * 1024 * 1024
        ),
    )(coefficients, profile_basis, psf, seen)
    grad = jnp.dot(
        tau.reshape(rows * cols, waves), profile_basis.T, preferred_element_type=jnp.float32
    )
    return grad.astype(jnp.bfloat16).reshape(rows, cols, profiles)


def solution(mesh):
    placed = (P("tile", "wave", None), P(), P(), P(None, "tile", "wave"))
    return jax.shard_map(
        functools.partial(shards, mesh.shape["tile"], mesh.shape["wave"]),
        mesh=mesh, in_specs=placed, out_specs=P("tile", "wave", None), check_vma=False,
    )
```
